32 devices in a mesh: ctx: 8 (over y, x, core), vocab: 4 (over z).
Axes of the slice: x: 2, y: 2, z: 4, core: 2. Of those that a mesh axis runs over, the one named last changes fastest.
Arguments:
- query_rows: bfloat16 [2048, 4096], P('ctx', 'vocab'), may hold values from -12 to 12
- key_rows: bfloat16 [2048, 2048], P('ctx', 'vocab'), may hold values from -6 to 6
- value_rows: bfloat16 [2048, 2048], P('ctx', 'vocab'), may hold values from -6 to 6
- residual: bfloat16 [2048, 4608], P('ctx', 'vocab'), may hold values from -6 to 6
- out_weight: bfloat16 [4096, 4608], P('vocab'), may hold values from -0.09375 to 0.09375
- post_gain: float32 [4608], P('vocab'), may hold values from 0.1 to 1.9
- final_gain: float32 [4608], P('vocab'), may hold values from 0.1 to 1.9
- embedding: bfloat16 [32768, 4608], P(('ctx', 'vocab')), may hold values from -0.25 to 0.25
- targets: int32 [64], P('ctx'), may hold values from 0 to 32767
- loss_mask: int32 [64], P('ctx'), may hold values 0 or 1
- pick_pos: int32 [64], P('ctx'), may hold values from 0 to 255, as said below
Outputs:
- final_hidden: bfloat16 [2048, 4608], P('ctx', 'vocab')
- mean_loss: float32 [], replicated
- grad_normed: float32 [64, 4608], P('ctx', 'vocab')
The draws below stay inside these ranges and needn't reach their ends.
Inputs may be any that keep to these rules, and one draw needn't show every extreme that they name: `pick_pos`: entry k is a position inside the block of 256 tokens held by index k // 8 of ctx; entries may repeat.
All inputs are finite; a program needn't handle non-finite values. No bound on the sum of `loss_mask` on one device may be relied on, other than what follows from the above.
Results may differ from the reference program's by a relative error of at most 0.0049.
Values may be sent and summed in bfloat16 or wider, within the bound.
A program may use at most 256 MiB of HBM per device.

```python
import math
import jax
import jax.numpy as jnp
import numpy as np
from jax import lax

D = 4608
HEADS = 32
KV_HEADS = 16
HEAD_DIM = 128
WINDOW = 4096
TOK_DEV = 256
PICK = 8
TOKENS = 2048
STRETCH = 64
VOCAB = 32768


def draw_pick_pos(key, part):
    values = jax.random.randint(key, (STRETCH,), 0, TOK_DEV, dtype=jnp.int32)
    values = values.at[0].set(0)
    return values.at[1].set(TOK_DEV - 1)


def plant(values, own_key, smallest, top_value):
    shape = values.shape
    index_at = [jax.random.randint(jax.random.fold_in(own_key, axis), (), 0, shape[axis]) for axis in range(len(shape))]
    values = values.at[tuple(index_at)].set(smallest)
    longest = shape.index(max(shape))
    index_at[longest] = (index_at[longest] + 1) % shape[longest]
    return values.at[tuple(index_at)].set(top_value)


def block_levels(stream_key, shape, cuts, smallest, top_value):
    factor_of = 1.0
    for axis_at, parts in cuts:
        steps = jax.random.uniform(jax.random.fold_in(jax.random.fold_in(stream_key, 6), axis_at), (parts,), jnp.float32, smallest / len(cuts), top_value / len(cuts))
        factor_of = factor_of * jnp.repeat(jnp.exp(steps), shape[axis_at] // parts).reshape((-1,) + (1,) * (len(shape) - 1 - axis_at))
    return factor_of


def cumulative_ranks(amount, slope):
    portions = [(1 << 20) // math.isqrt(grade ** slope) + 1 for grade in range(1, amount + 1)]
    spread = 1 + sum(portions) // (1 << 30)
    return np.cumsum(np.array([max(1, weight // spread) for weight in portions]))


def ranked_ids(key, extent, number_of, slope):
    listing = cumulative_ranks(number_of, slope)
    pick = jax.random.randint(jax.random.fold_in(key, 1), extent, 0, int(listing[number_of - 1]))
    rank = jnp.searchsorted(jnp.asarray(listing, jnp.int32), pick, side="right")
    return jax.random.permutation(jax.random.fold_in(key, 2), number_of)[rank].astype(jnp.int32)


def noise(own_key, shape, spread, limit, shards=(), held_as=jnp.bfloat16):
    drawn = jax.random.normal(own_key, shape, jnp.float32) * spread
    if len(shards) > 0:
        drawn = block_levels(own_key, shape, shards, -0.22, 0.18) * drawn
    return jnp.clip(drawn, min=-limit, max=limit).astype(held_as)


def setup_inputs(seed: int = 0) -> dict:
    keys = jax.random.split(jax.random.key(seed), 12)
    query_rows = noise(keys[0], (TOKENS, HEADS * HEAD_DIM), 3.0, 12.0, ((0, 8), (1, 4)))
    key_rows = noise(keys[1], (TOKENS, KV_HEADS * HEAD_DIM), 1.0, 6.0, ((0, 8), (1, 4)))
    value_rows = noise(keys[2], (TOKENS, KV_HEADS * HEAD_DIM), 1.0, 6.0, ((0, 8), (1, 4)))
    residual = noise(keys[3], (TOKENS, D), 1.0, 6.0, ((0, 8), (1, 4)))
    out_weight = noise(keys[4], (HEADS * HEAD_DIM, D), (HEADS * HEAD_DIM) ** -0.5, 0.09375, ((0, 4),))
    post_gain = jnp.clip(1.0 + 0.18 * jax.random.normal(keys[5], (D,), jnp.float32), 0.1, 1.9)
    final_gain = jnp.clip(1.0 + 0.18 * jax.random.normal(keys[6], (D,), jnp.float32), 0.1, 1.9)
    embedding = noise(keys[7], (VOCAB, D), (D // 9) ** -0.5, 0.25, ((0, 32),))
    targets = plant(ranked_ids(keys[8], (STRETCH,), VOCAB, 2), jax.random.fold_in(keys[8], 3), 0, VOCAB - 1).astype(jnp.int32)
    loss_mask = plant((jax.random.randint(keys[9], (STRETCH,), 0, 8) < 7).astype(jnp.int32), jax.random.fold_in(keys[9], 1), 0, 1)
    pick_pos = draw_pick_pos(jax.random.fold_in(keys[11], 71), 0)
    return dict(query_rows=query_rows, key_rows=key_rows, value_rows=value_rows, residual=residual, out_weight=out_weight, post_gain=post_gain, final_gain=final_gain, embedding=embedding, targets=targets, loss_mask=loss_mask, pick_pos=pick_pos)


attn_cap = 50.0
logit_cap = 30.0
query_scalar = 144.0
epsilon = 1e-06

def attend_block(block_idx, query_rows, key_rows, value_rows):
    key_span = min(TOKENS, WINDOW + TOK_DEV)
    group_size = HEADS // KV_HEADS
    first_row = (block_idx * TOK_DEV).astype(jnp.int32)
    begin_row = jnp.clip(first_row + TOK_DEV - key_span, 0, TOKENS - key_span).astype(jnp.int32)
    query_blk = lax.dynamic_slice_in_dim(query_rows, first_row, TOK_DEV, 0).astype(jnp.float32)
    query_blk = query_blk.reshape(TOK_DEV, KV_HEADS, group_size, HEAD_DIM)
    key_blk = lax.dynamic_slice_in_dim(key_rows, begin_row, key_span, 0).astype(jnp.float32)
    key_blk = key_blk.reshape(key_span, KV_HEADS, HEAD_DIM)
    value_blk = lax.dynamic_slice_in_dim(value_rows, begin_row, key_span, 0).astype(jnp.float32)
    value_blk = value_blk.reshape(key_span, KV_HEADS, HEAD_DIM)
    raw_scores = jnp.einsum('tgcd,sgd->gcts', query_blk, key_blk)
    capped = attn_cap * jnp.tanh(raw_scores * query_scalar ** (-0.5) / attn_cap)
    query_pos = first_row + jnp.arange(TOK_DEV, dtype=jnp.int32)
    key_pos = begin_row + jnp.arange(key_span, dtype=jnp.int32)
    distance = query_pos[:, None] - key_pos[None, :]
    allowed = (distance >= 0) & (distance < WINDOW)
    weights = jnp.where(allowed, jnp.exp(capped), 0.0)
    denominator = lax.optimization_barrier(jnp.sum(weights, axis=-1))
    weights_low = lax.optimization_barrier(weights.astype(jnp.bfloat16)).astype(jnp.float32)
    numerator = jnp.einsum('gcts,sgd->gctd', weights_low, value_blk)
    attended = numerator / denominator[..., None]
    attended = jnp.transpose(attended, (2, 0, 1, 3)).reshape(TOK_DEV, HEADS * HEAD_DIM)
    return attended.astype(jnp.bfloat16)

def reference(query_rows, key_rows, value_rows, residual, out_weight, post_gain, final_gain, embedding, targets, loss_mask, pick_pos):

    def one_block(block_idx):
        return attend_block(block_idx, query_rows, key_rows, value_rows)
    attended = lax.map(one_block, jnp.arange(TOKENS // TOK_DEV, dtype=jnp.int32))
    attended = attended.reshape(TOKENS, HEADS * HEAD_DIM)
    projected = jnp.dot(attended, out_weight, preferred_element_type=jnp.float32)
    inv_rms = lax.rsqrt(lax.optimization_barrier(jnp.mean(projected * projected, axis=1, keepdims=True)) + epsilon)
    final_hidden = (residual.astype(jnp.float32) + projected * inv_rms * post_gain).astype(jnp.bfloat16)
    row_index = jnp.arange(STRETCH, dtype=jnp.int32) // PICK * TOK_DEV + pick_pos.astype(jnp.int32)
    picked = jnp.take(final_hidden, row_index, axis=0).astype(jnp.float32)
    picked_rms = lax.rsqrt(lax.optimization_barrier(jnp.mean(picked * picked, axis=1, keepdims=True)) + epsilon)
    normed = (picked * picked_rms * final_gain).astype(jnp.bfloat16)
    logits = jnp.dot(normed, embedding.T, preferred_element_type=jnp.float32)
    logits = logit_cap * jnp.tanh(logits / logit_cap)
    exp_logits = jnp.exp(logits)
    totals = lax.optimization_barrier(jnp.sum(exp_logits, axis=1))
    onehot = jnp.arange(VOCAB, dtype=jnp.int32)[None, :] == targets[:, None]
    target_logit = lax.optimization_barrier(jnp.sum(jnp.where(onehot, logits, 0.0), axis=1))
    mask_float = loss_mask.astype(jnp.float32)
    mean_loss = jnp.sum(mask_float * (jnp.log(totals) - target_logit)) / STRETCH
    dlogits = mask_float[:, None] * (exp_logits / totals[:, None] - onehot.astype(jnp.float32))
    dlogits = (dlogits * (1.0 - (logits / logit_cap) ** 2)).astype(jnp.bfloat16)
    grad_normed = jnp.dot(dlogits, embedding, preferred_element_type=jnp.float32)
    return (final_hidden, mean_loss, grad_normed)
```

```python
import functools
import math

import jax
import jax.numpy as jnp
from jax import lax
from jax.experimental import pallas as pl
from jax.experimental.pallas import tpu as pltpu
from jax.sharding import PartitionSpec as P

D = 4608
HEADS = 32
KV_HEADS = 16
HEAD_DIM = 128
WINDOW = 4096


attn_cap = 50.0
logit_cap = 30.0
query_scalar = 144.0
epsilon = 1e-06
MESH = pl.DeviceIdType.MESH


def attend(key_value, query_grp, query_pos):
    piece_len = key_value.shape[1]
    kv_local = query_grp.shape[1]
    key_piece = key_value[0].reshape(piece_len, kv_local, HEAD_DIM)
    value_piece = key_value[1].reshape(piece_len, kv_local, HEAD_DIM)
    raw_scores = jnp.einsum(
        "tgcd,sgd->gcts", query_grp, key_piece, preferred_element_type=jnp.float32
    )
    capped = attn_cap * jnp.tanh(raw_scores * query_scalar ** (-0.5) / attn_cap)
    key_pos = jnp.arange(piece_len, dtype=jnp.int32)
    distance = query_pos[:, None] - key_pos[None, :]
    allowed = (distance >= 0) & (distance < WINDOW) & (key_pos[None, :] >= 0)
    weights = jnp.where(allowed, jnp.exp(capped), 0.0)
    acc_weights = jnp.sum(weights, axis=-1)
    acc_values = jnp.einsum(
        "gcts,sgd->gctd",
        weights.astype(jnp.bfloat16),
        value_piece,
        preferred_element_type=jnp.float32,
    )
    return (acc_values, acc_weights)


def shards(
    query_rows,
    key_rows,
    value_rows,
    residual,
    out_weight,
    post_gain,
    final_gain,
    embedding,
    targets,
    loss_mask,
    pick_pos,
):
    local_len = query_rows.shape[0]
    group_size = HEADS // KV_HEADS
    kv_local = key_rows.shape[1] // HEAD_DIM
    ctx_index = lax.axis_index("ctx")
    query_grp = query_rows.reshape(local_len, kv_local, group_size, HEAD_DIM)
    query_pos = ctx_index * local_len + jnp.arange(local_len, dtype=jnp.int32)
    key_value = jnp.stack((key_rows, value_rows))
    initial = (
        jnp.zeros((kv_local, group_size, local_len, HEAD_DIM), jnp.float32),
        jnp.zeros((kv_local, group_size, local_len), jnp.float32),
    )
    first_query = ctx_index * local_len
    last_query = first_query + local_len - 1
    piece = lax.all_gather(key_value, "ctx", axis=1, tiled=True)
    offset = jnp.int32(0)
    piece_len = piece.shape[1]
    needed = (offset <= last_query) & (offset + piece_len - 1 > first_query - WINDOW)

    def work(state_now):
        return attend(piece, query_grp, query_pos)

    def skip(state_now):
        return state_now

    acc_values, acc_weights = lax.cond(needed, work, skip, initial)
    attended = acc_values / acc_weights[..., None]
    attended = jnp.transpose(attended, (2, 0, 1, 3)).reshape(
        local_len, kv_local * group_size * HEAD_DIM
    )
    attended = attended.astype(jnp.bfloat16)
    partial_proj = jnp.dot(attended, out_weight, preferred_element_type=jnp.float32)
    own_cols = lax.psum_scatter(partial_proj, "vocab", scatter_dimension=1, tiled=True)
    square_sum = lax.psum(jnp.sum(own_cols * own_cols, axis=1, keepdims=True), "vocab")
    inv_rms = lax.rsqrt(square_sum / D + epsilon)
    final_hidden = (residual.astype(jnp.float32) + own_cols * inv_rms * post_gain).astype(
        jnp.bfloat16
    )
    picked = jnp.take(final_hidden, pick_pos, axis=0).astype(jnp.float32)
    picked_sum = lax.psum(jnp.sum(picked * picked, axis=1, keepdims=True), "vocab")
    normed = (picked * lax.rsqrt(picked_sum / D + epsilon) * final_gain).astype(jnp.bfloat16)
    normed_full = lax.all_gather(normed, "vocab", axis=1, tiled=True)
    all_targets, all_mask = (
        lax.all_gather(targets, "ctx", axis=0, tiled=True),
        lax.all_gather(loss_mask, "ctx", axis=0, tiled=True),
    )
    raw_logits = jnp.einsum(
        "td,vd->tv",
        lax.all_gather(normed_full, "ctx", axis=0, tiled=True),
        embedding,
        preferred_element_type=jnp.float32,
    )
    logits = logit_cap * jnp.tanh(raw_logits / logit_cap)
    vocab_local = embedding.shape[0]
    vocab_base = (ctx_index * lax.axis_size("vocab") + lax.axis_index("vocab")) * vocab_local
    onehot = (vocab_base + jnp.arange(vocab_local, dtype=jnp.int32))[None, :] == all_targets[
        :, None
    ]
    exp_logits = jnp.exp(logits)
    local_total = jnp.sum(exp_logits, axis=1)
    local_target = jnp.sum(jnp.where(onehot, logits, 0.0), axis=1)
    totals, target_logit = lax.psum((local_total, local_target), ("ctx", "vocab"))
    mask_float = all_mask.astype(jnp.float32)
    mean_loss = jnp.sum(mask_float * (jnp.log(totals) - target_logit)) / all_targets.shape[0]
    dlogits = mask_float[:, None] * (exp_logits / totals[:, None] - onehot.astype(jnp.float32))
    dlogits = (dlogits * (1.0 - (logits / logit_cap) ** 2)).astype(jnp.bfloat16)
    partial_grad = jnp.dot(dlogits, embedding, preferred_element_type=jnp.float32)
    by_features = lax.psum_scatter(partial_grad, "vocab", scatter_dimension=1, tiled=True)
    grad_normed = lax.psum_scatter(by_features, "ctx", scatter_dimension=0, tiled=True)
    return (final_hidden, mean_loss, grad_normed)


def flip(index, offset):
    moved, bit = 0, 1
    while bit <= offset or bit == 1:
        here = lax.rem(index // bit, 2)
        moved = moved + bit * (lax.rem(here + (offset // bit) % 2, 2) - here)
        bit *= 2
    return index + moved


def fused_kernel(
    n, vn, q, k, v, res, w_hbm, post, final, e_hbm, tm, pos,
    hid_out, loss_out, grad_out,
    q_all, k_all, v_all, out_all, att, w_buf, e_buf, part, own, up, down, sq_all, pick_z, gain_z,
    pick_all, tm_all, tot_z, tot_p, gsend, grecv, zsend, zrecv, acc,
    w_sem, e_sem, qs, qr, ks, kr, vs, vr, fks, fkr, fvs, fvr, outs, outr, ups, upr, dns, dnr,
    sqs, sqr, pzs, pzr, gns, gnr, pas, par, tms, tmr, tzs, tzr, tps, tpr, gs, gr, zs, zr,
):
    me, z = lax.axis_index("ctx"), lax.axis_index("vocab")
    tok, feat = res.shape
    model = vn * feat
    half = model // 2
    picks = tm.shape[0]
    total_picks = n * picks
    vocab_local = e_buf.shape[0]
    chunks = ups.shape[1]
    rows = tok // chunks
    f32 = jnp.float32

    def plane(i):
        return {"ctx": i, "vocab": z}

    def column(i):
        return {"ctx": me, "vocab": i}

    def copy(src, dst, send, recv, device):
        return pltpu.make_async_remote_copy(
            src_ref=src, dst_ref=dst, send_sem=send, recv_sem=recv,
            device_id=device, device_id_type=MESH,
        )

    def lanes(i):
        return pl.ds(pl.multiple_of(i * HEAD_DIM, HEAD_DIM), HEAD_DIM)

    barrier = pltpu.get_barrier_semaphore()
    for off in range(1, n):
        pl.semaphore_signal(barrier, inc=1, device_id=plane(flip(me, off)), device_id_type=MESH)
    for off in range(1, vn):
        pl.semaphore_signal(
            barrier, inc=1, device_id=column(lax.rem(z + off, vn)), device_id_type=MESH
        )
    w_copy = pltpu.make_async_copy(w_hbm, w_buf, w_sem)
    w_copy.start()
    chip = me // 2
    sibling = flip(me, 1)
    q_all[pl.ds(me, 1)] = q[:, lanes(me)][None]
    k_all[pl.ds(me, 1)] = k[:, lanes(chip)][None]
    v_all[pl.ds(me, 1)] = v[:, lanes(chip)][None]
    pl.semaphore_wait(barrier, n + vn - 2)

    kv_copies, q_copies, small = {}, {}, []
    for off in (*range(2, n, 2), 1):
        peer = flip(me, off)
        kv_copies[off] = (
            copy(k.at[:, lanes(peer // 2)], k_all.at[me], ks.at[off], kr.at[off], plane(peer)),
            copy(v.at[:, lanes(peer // 2)], v_all.at[me], vs.at[off], vr.at[off], plane(peer)),
        )
        for c in kv_copies[off]:
            c.start()
    for off in range(1, n):
        peer = flip(me, off)
        c = copy(q.at[:, lanes(peer)], q_all.at[me], qs.at[off], qr.at[off], plane(peer))
        c.start()
        q_copies[off] = c
    e_copy = pltpu.make_async_copy(e_hbm, e_buf, e_sem)
    e_copy.start()
    for off in range(1, n):
        peer = flip(me, off)
        c = copy(tm, tm_all.at[me], tms.at[off], tmr.at[off], plane(peer))
        c.start()
        small.append(c)
    for off in range(1, vn):
        c = copy(final, gain_z.at[z], gns.at[off], gnr.at[off], column(lax.rem(z + off, vn)))
        c.start()
        small.append(c)
    tm_all[pl.ds(me, 1)] = tm[...][None]
    gain_z[pl.ds(z, 1)] = final[...][None]
    forwards = []
    for off in range(2, n, 2):
        source = flip(me, off)
        for c in kv_copies[off]:
            c.wait_recv()
        pair = (
            copy(k_all.at[source], k_all.at[source], fks.at[off], fkr.at[off], plane(sibling)),
            copy(v_all.at[source], v_all.at[source], fvs.at[off], fvr.at[off], plane(sibling)),
        )
        for c in pair:
            c.start()
        forwards.extend(pair)
    for c in kv_copies[1]:
        c.wait_recv()
    for off in range(1, n):
        q_copies[off].wait_recv()
    for c in forwards:
        c.wait_recv()

    row_id = lax.broadcasted_iota(jnp.int32, (tok, tok), 0)
    col_id = lax.broadcasted_iota(jnp.int32, (tok, tok), 1)
    causal = row_id >= col_id
    pre = query_scalar ** (-0.5) / attn_cap
    post_scale = attn_cap * math.log2(math.e)

    def out_copy(i):
        return copy(out_all.at[i], att.at[:, lanes(me)], outs.at[i], outr.at[me], plane(i))

    for i in range(n - 1, -1, -1):
        query = q_all[i]
        total = jnp.zeros((tok, 1), f32)
        values = jnp.zeros((tok, HEAD_DIM), f32)
        for j in range(i + 1):
            s = lax.dot_general(
                query, k_all[j], (((1,), (1,)), ((), ())), preferred_element_type=f32
            )
            w = jnp.exp2(jnp.tanh(s * pre) * post_scale)
            if j == i:
                w = jnp.where(causal, w, 0.0)
            total = total + jnp.sum(w, axis=1, keepdims=True)
            values = values + jnp.dot(w.astype(jnp.bfloat16), v_all[j], preferred_element_type=f32)
        out_all[i] = (values / total).astype(jnp.bfloat16)

        @pl.when(me == i)
        def _():
            att[:, i * HEAD_DIM : (i + 1) * HEAD_DIM] = out_all[i]

        @pl.when(me != i)
        def _():
            out_copy(i).start()

    w_copy.wait()
    for i in range(n):

        @pl.when(me != i)
        def _():
            copy(
                out_all.at[i], att.at[:, lanes(i)], outs.at[i], outr.at[i], plane(i)
            ).wait_recv()

    def up_copy(dst, r, source):
        at = pl.ds(r * rows, rows)
        return copy(
            source.at[dst, at], up.at[dst, at], ups.at[dst, r], upr.at[dst, r],
            column(jnp.minimum(z + 1, vn - 1)),
        )

    def down_copy(dst, r, source):
        at = pl.ds(r * rows, rows)
        return copy(
            source.at[dst, at], down.at[dst, at], dns.at[dst, r], dnr.at[dst, r],
            column(jnp.maximum(z - 1, 0)),
        )

    order = []
    for t in range(vn):
        for d in (vn - 1 - t, t):
            if d not in order:
                order.append(d)
    for dst in order:
        product = jnp.dot(
            att[...], w_buf[:, dst * feat : (dst + 1) * feat], preferred_element_type=f32
        )

        @pl.when(z == dst)
        def _():
            own[...] = product

        @pl.when(z != dst)
        def _():
            part[dst] = product.astype(jnp.bfloat16)

        if dst > 0:

            @pl.when(z == 0)
            def _():
                for r in range(chunks):
                    up_copy(dst, r, part).start()

        if dst < vn - 1:

            @pl.when(z == vn - 1)
            def _():
                for r in range(chunks):
                    down_copy(dst, r, part).start()

    for t in range(vn):
        d_up, d_down = vn - 1 - t, t
        for r in range(chunks):
            at = pl.ds(r * rows, rows)
            if 1 < d_up:

                @pl.when((z > 0) & (z < d_up))
                def _():
                    up_copy(d_up, r, up).wait_recv()
                    up[d_up, at] = (up[d_up, at].astype(f32) + part[d_up, at].astype(f32)).astype(
                        jnp.bfloat16
                    )
                    up_copy(d_up, r, up).start()

            if d_down < vn - 2:

                @pl.when((z < vn - 1) & (z > d_down))
                def _():
                    down_copy(d_down, r, down).wait_recv()
                    down[d_down, at] = (
                        down[d_down, at].astype(f32) + part[d_down, at].astype(f32)
                    ).astype(jnp.bfloat16)
                    down_copy(d_down, r, down).start()

    for dst in range(vn):

        @pl.when(z == dst)
        def _():
            for r in range(chunks):
                at = pl.ds(r * rows, rows)
                value = own[at]
                if dst > 0:
                    up_copy(dst, r, up).wait_recv()
                    value = value + up[dst, at].astype(f32)
                if dst < vn - 1:
                    down_copy(dst, r, down).wait_recv()
                    value = value + down[dst, at].astype(f32)
                own[at] = value

    cols = own[...]
    squares = jnp.sum(cols * cols, axis=1, keepdims=True)
    wide = jnp.transpose(jnp.broadcast_to(squares, (tok, 128)))
    sq_all[pl.ds(z, 1)] = wide[:8][None]
    sq_copies = []
    for off in range(1, vn):
        c = copy(
            sq_all.at[z], sq_all.at[z], sqs.at[off], sqr.at[off], column(lax.rem(z + off, vn))
        )
        c.start()
        sq_copies.append(c)
    for c in sq_copies:
        c.wait_recv()
    summed = jnp.sum(sq_all[...], axis=0)[:1]
    inv = lax.rsqrt(summed / model + epsilon)
    inv = jnp.transpose(jnp.broadcast_to(inv, (128, tok)))[:, :1]
    hidden = (res[...].astype(f32) + cols * inv * post[...]).astype(jnp.bfloat16)
    hid_out[...] = hidden
    chosen = pos[...] == lax.broadcasted_iota(jnp.int32, (picks, tok), 1)
    picked = jnp.dot(chosen.astype(f32).astype(jnp.bfloat16), hidden, preferred_element_type=f32)
    pick_z[pl.ds(z, 1)] = picked[None]
    pz_copies = []
    for off in range(1, vn):
        c = copy(
            pick_z.at[z], pick_z.at[z], pzs.at[off], pzr.at[off], column(lax.rem(z + off, vn))
        )
        c.start()
        pz_copies.append(c)
    for c in pz_copies:
        c.wait_recv()
    for c in small:
        c.wait_recv()
    whole = jnp.concatenate([pick_z[i] for i in range(vn)], axis=1)
    gain = jnp.concatenate([gain_z[i] for i in range(vn)], axis=1)
    scale = lax.rsqrt(jnp.sum(whole * whole, axis=1, keepdims=True) / model + epsilon)
    normed = whole * scale * gain
    pick_all[pl.ds(me, 1)] = (
        jnp.concatenate([normed[:, :half], normed[:, half:]], axis=0).astype(jnp.bfloat16)[None]
    )
    pa_copies = {}
    for off in (*range(2, n, 2), 1):
        pa_copies[off] = copy(
            pick_all.at[me], pick_all.at[me], pas.at[off], par.at[off], plane(flip(me, off))
        )
        pa_copies[off].start()
    passed = []
    for off in range(2, n, 2):
        source = flip(me, off)
        pa_copies[off].wait_recv()
        c = copy(
            pick_all.at[source], pick_all.at[source], pas.at[off + 1], par.at[off + 1],
            plane(sibling),
        )
        c.start()
        passed.append(c)
    pa_copies[1].wait_recv()
    for c in passed:
        c.wait_recv()
    e_copy.wait()
    left, right = [], []
    for i in range(n):
        block = pick_all[i].astype(f32)
        left.append(block[:picks])
        right.append(block[picks:])
    states = jnp.concatenate(
        [jnp.concatenate(left, axis=0), jnp.concatenate(right, axis=0)], axis=1
    ).astype(jnp.bfloat16)
    raw = lax.dot_general(
        states, e_buf[...], (((1,), (1,)), ((), ())), preferred_element_type=f32
    )
    ratio = jnp.tanh(raw / logit_cap)
    logits = logit_cap * ratio
    tm_rows = tm_all[...].reshape(total_picks, 128)
    target = tm_rows[:, :1]
    mask = tm_rows[:, 64:65].astype(f32)
    base = (me * vn + z) * vocab_local
    onehot = base + lax.broadcasted_iota(jnp.int32, (total_picks, vocab_local), 1) == target
    exp_logits = jnp.exp(logits)
    slope = 1.0 - ratio * ratio
    local_total = jnp.sum(exp_logits, axis=1, keepdims=True)
    local_target = jnp.sum(jnp.where(onehot, logits, 0.0), axis=1, keepdims=True)
    target_slope = jnp.sum(jnp.where(onehot, slope, 0.0), axis=1, keepdims=True)
    target_exp = jnp.sum(jnp.where(onehot, exp_logits, 0.0), axis=1, keepdims=True)
    lane = lax.broadcasted_iota(jnp.int32, (total_picks, 128), 1)
    packed = jnp.where(lane == 0, local_total, jnp.where(lane == 1, local_target, 0.0))
    packed = jnp.concatenate([packed, jnp.zeros((128 - total_picks, 128), f32)], axis=0)
    tot_z[pl.ds(z, 1)] = jnp.transpose(packed)[:8][None]
    tz_copies = []
    for off in range(1, vn):
        c = copy(tot_z.at[z], tot_z.at[z], tzs.at[off], tzr.at[off], column(lax.rem(z + off, vn)))
        c.start()
        tz_copies.append(c)
    weights = jnp.concatenate(
        [jnp.where(onehot, 0.0, exp_logits * slope), jnp.where(onehot, 1.0, 0.0)], axis=0
    ).astype(jnp.bfloat16)
    for c in tz_copies:
        c.wait_recv()
    tot_p[pl.ds(me, 1)] = jnp.sum(tot_z[...], axis=0)[None]
    tp_copies = []
    for off in range(1, n):
        c = copy(tot_p.at[me], tot_p.at[me], tps.at[off], tpr.at[off], plane(flip(me, off)))
        c.start()
        tp_copies.append(c)
    acc[...] = jnp.dot(weights, e_buf[...], preferred_element_type=f32)
    for c in tp_copies:
        c.wait_recv()
    sums = jnp.sum(tot_p[...], axis=0)
    sums = jnp.transpose(jnp.concatenate([sums, jnp.zeros((120, 128), f32)], axis=0))
    totals = sums[:total_picks, :1]
    target_logit = sums[:total_picks, 1:2]
    loss = jnp.sum(mask * (jnp.log(totals) - target_logit), axis=0, keepdims=True) / total_picks
    loss_out[...] = jnp.broadcast_to(loss, loss_out.shape)
    other = mask / totals
    at_target = (mask * (target_exp / totals - 1.0) * target_slope).astype(jnp.bfloat16).astype(f32)
    grad = other * acc[:total_picks] + at_target * acc[total_picks:]
    for i in range(n):
        block = grad[i * picks : (i + 1) * picks]
        gsend[i] = jnp.concatenate([block[:, :half], block[:, half:]], axis=0).astype(jnp.bfloat16)
    g_copies = []
    for off in (*range(2, n), 1):
        peer = flip(me, off)
        c = copy(gsend.at[peer], grecv.at[me], gs.at[off], gr.at[off], plane(peer))
        c.start()
        g_copies.append(c)
    grecv[pl.ds(me, 1)] = gsend[pl.ds(me, 1)]
    for c in g_copies:
        c.wait_recv()
    both = grecv[0].astype(f32)
    for i in range(1, n):
        both = both + grecv[i].astype(f32)
    mine = jnp.concatenate([both[:picks], both[picks:]], axis=1)
    for i in range(vn):
        zsend[i] = mine[:, i * feat : (i + 1) * feat]
    z_copies = []
    for off in range(1, vn):
        peer = lax.rem(z + off, vn)
        c = copy(zsend.at[peer], zrecv.at[z], zs.at[off], zr.at[off], column(peer))
        c.start()
        z_copies.append(c)
    zrecv[pl.ds(z, 1)] = zsend[pl.ds(z, 1)]
    for c in z_copies:
        c.wait_recv()
    grad_out[...] = jnp.sum(zrecv[...], axis=0)

    for pair in kv_copies.values():
        for c in pair:
            c.wait_send()
    for group in (
        q_copies.values(), small, forwards, sq_copies, pz_copies, pa_copies.values(), passed,
        tz_copies, tp_copies, g_copies, z_copies,
    ):
        for c in group:
            c.wait_send()
    for i in range(n):

        @pl.when(me != i)
        def _():
            out_copy(i).wait_send()

    for dst in range(vn):
        for r in range(chunks):

            @pl.when(z < dst)
            def _():
                up_copy(dst, r, up).wait_send()

            @pl.when(z > dst)
            def _():
                down_copy(dst, r, down).wait_send()


def fused(
    n, vn, query_rows, key_rows, value_rows, residual, out_weight, post_gain, final_gain,
    embedding, targets, loss_mask, pick_pos,
):
    tok, feat = residual.shape
    model = vn * feat
    picks = targets.shape[0]
    bf16, f32, i32 = jnp.bfloat16, jnp.float32, jnp.int32
    chunks = 4
    first = jnp.broadcast_to(targets[:, None], (picks, 64))
    second = jnp.broadcast_to(loss_mask[:, None], (picks, 64))
    tm = jnp.concatenate([first, second], axis=1)
    dma = pltpu.SemaphoreType.DMA
    vmem = pl.BlockSpec(memory_space=pltpu.VMEM)
    hbm = pl.BlockSpec(memory_space=pl.ANY)
    sems = [dma, dma] + [dma((n,))] * 12 + [dma((vn, chunks))] * 4 + [dma((vn,))] * 6
    sems += [dma((n,))] * 4 + [dma((vn,))] * 2 + [dma((n,))] * 4 + [dma((vn,))] * 2
    hidden, loss, grad = pl.pallas_call(
        functools.partial(fused_kernel, n, vn),
        out_shape=(
            jax.ShapeDtypeStruct((tok, feat), bf16),
            jax.ShapeDtypeStruct((8, 128), f32),
            jax.ShapeDtypeStruct((picks, feat), f32),
        ),
        in_specs=[vmem, vmem, vmem, vmem, hbm, vmem, vmem, hbm, vmem, vmem],
        out_specs=(vmem, vmem, vmem),
        scratch_shapes=[
            pltpu.VMEM((n, tok, HEAD_DIM), bf16),
            pltpu.VMEM((n, tok, HEAD_DIM), bf16),
            pltpu.VMEM((n, tok, HEAD_DIM), bf16),
            pltpu.VMEM((n, tok, HEAD_DIM), bf16),
            pltpu.VMEM((tok, n * HEAD_DIM), bf16),
            pltpu.VMEM(out_weight.shape, bf16),
            pltpu.VMEM(embedding.shape, bf16),
            pltpu.VMEM((vn, tok, feat), bf16),
            pltpu.VMEM((tok, feat), f32),
            pltpu.VMEM((vn, tok, feat), bf16),
            pltpu.VMEM((vn, tok, feat), bf16),
            pltpu.VMEM((vn, 8, tok), f32),
            pltpu.VMEM((vn, picks, feat), f32),
            pltpu.VMEM((vn, picks, feat), f32),
            pltpu.VMEM((n, 2 * picks, model // 2), bf16),
            pltpu.VMEM((n, picks, 128), i32),
            pltpu.VMEM((vn, 8, 128), f32),
            pltpu.VMEM((n, 8, 128), f32),
            pltpu.VMEM((n, 2 * picks, model // 2), bf16),
            pltpu.VMEM((n, 2 * picks, model // 2), bf16),
            pltpu.VMEM((vn, picks, feat), f32),
            pltpu.VMEM((vn, picks, feat), f32),
            pltpu.VMEM((2 * n * picks, model), f32),
            *sems,
        ],
        compiler_params=pltpu.CompilerParams(
            collective_id=0, has_side_effects=True, vmem_limit_bytes=60 * 1024 * 1024
        ),
    )(
        query_rows, key_rows, value_rows, residual, out_weight, post_gain[None, :],
        jnp.broadcast_to(final_gain[None, :], (picks, feat)), embedding, tm, pick_pos[:, None],
    )
    return hidden, loss[0, 0], grad


def fits(n, vn, query_rows, key_rows, residual, targets):
    heads, kv = query_rows.shape[1] // HEAD_DIM, key_rows.shape[1] // HEAD_DIM
    tok, feat = residual.shape
    return (
        n >= 2
        and n & (n - 1) == 0
        and heads == n
        and heads == 2 * kv
        and vn >= 2
        and n * tok <= WINDOW
        and tok % 128 == 0
        and feat % 128 == 0
        and (vn * feat) % 256 == 0
        and targets.shape[0] == 8
        and n * targets.shape[0] <= 128
    )


def solution(mesh):
    in_specs = (
        P("ctx", "vocab"),
        P("ctx", "vocab"),
        P("ctx", "vocab"),
        P("ctx", "vocab"),
        P("vocab", None),
        P("vocab"),
        P("vocab"),
        P(("ctx", "vocab"), None),
        P("ctx"),
        P("ctx"),
        P("ctx"),
    )
    out_specs = (P("ctx", "vocab"), P(), P("ctx", "vocab"))
    n, vn = mesh.shape["ctx"], mesh.shape["vocab"]

    def local(*args):
        if fits(n, vn, args[0], args[1], args[3], args[8]):
            return fused(n, vn, *args)
        return shards(*args)

    return jax.shard_map(local, mesh=mesh, in_specs=in_specs, out_specs=out_specs, check_vma=False)
```

```python
import functools
import math

import jax
import jax.numpy as jnp
from jax import lax
from jax.experimental import pallas as pl
from jax.experimental.pallas import tpu as pltpu
from jax.sharding import PartitionSpec as P

D = 4608
HEADS = 32
KV_HEADS = 16
HEAD_DIM = 128
WINDOW = 4096


attn_cap = 50.0
logit_cap = 30.0
query_scalar = 144.0
epsilon = 1e-06
MESH = pl.DeviceIdType.MESH


def attend(key_value, query_grp, query_pos):
    piece_len = key_value.shape[1]
    kv_local = query_grp.shape[1]
    key_piece = key_value[0].reshape(piece_len, kv_local, HEAD_DIM)
    value_piece = key_value[1].reshape(piece_len, kv_local, HEAD_DIM)
    raw_scores = jnp.einsum(
        "tgcd,sgd->gcts", query_grp, key_piece, preferred_element_type=jnp.float32
    )
    capped = attn_cap * jnp.tanh(raw_scores * query_scalar ** (-0.5) / attn_cap)
    key_pos = jnp.arange(piece_len, dtype=jnp.int32)
    distance = query_pos[:, None] - key_pos[None, :]
    allowed = (distance >= 0) & (distance < WINDOW) & (key_pos[None, :] >= 0)
    weights = jnp.where(allowed, jnp.exp(capped), 0.0)
    acc_weights = jnp.sum(weights, axis=-1)
    acc_values = jnp.einsum(
        "gcts,sgd->gctd",
        weights.astype(jnp.bfloat16),
        value_piece,
        preferred_element_type=jnp.float32,
    )
    return (acc_values, acc_weights)


def shards(
    query_rows,
    key_rows,
    value_rows,
    residual,
    out_weight,
    post_gain,
    final_gain,
    embedding,
    targets,
    loss_mask,
    pick_pos,
):
    local_len = query_rows.shape[0]
    group_size = HEADS // KV_HEADS
    kv_local = key_rows.shape[1] // HEAD_DIM
    ctx_index = lax.axis_index("ctx")
    query_grp = query_rows.reshape(local_len, kv_local, group_size, HEAD_DIM)
    query_pos = ctx_index * local_len + jnp.arange(local_len, dtype=jnp.int32)
    key_value = jnp.stack((key_rows, value_rows))
    initial = (
        jnp.zeros((kv_local, group_size, local_len, HEAD_DIM), jnp.float32),
        jnp.zeros((kv_local, group_size, local_len), jnp.float32),
    )
    first_query = ctx_index * local_len
    last_query = first_query + local_len - 1
    piece = lax.all_gather(key_value, "ctx", axis=1, tiled=True)
    offset = jnp.int32(0)
    piece_len = piece.shape[1]
    needed = (offset <= last_query) & (offset + piece_len - 1 > first_query - WINDOW)

    def work(state_now):
        return attend(piece, query_grp, query_pos)

    def skip(state_now):
        return state_now

    acc_values, acc_weights = lax.cond(needed, work, skip, initial)
    attended = acc_values / acc_weights[..., None]
    attended = jnp.transpose(attended, (2, 0, 1, 3)).reshape(
        local_len, kv_local * group_size * HEAD_DIM
    )
    attended = attended.astype(jnp.bfloat16)
    partial_proj = jnp.dot(attended, out_weight, preferred_element_type=jnp.float32)
    own_cols = lax.psum_scatter(partial_proj, "vocab", scatter_dimension=1, tiled=True)
    square_sum = lax.psum(jnp.sum(own_cols * own_cols, axis=1, keepdims=True), "vocab")
    inv_rms = lax.rsqrt(square_sum / D + epsilon)
    final_hidden = (residual.astype(jnp.float32) + own_cols * inv_rms * post_gain).astype(
        jnp.bfloat16
    )
    picked = jnp.take(final_hidden, pick_pos, axis=0).astype(jnp.float32)
    picked_sum = lax.psum(jnp.sum(picked * picked, axis=1, keepdims=True), "vocab")
    normed = (picked * lax.rsqrt(picked_sum / D + epsilon) * final_gain).astype(jnp.bfloat16)
    normed_full = lax.all_gather(normed, "vocab", axis=1, tiled=True)
    all_targets, all_mask = (
        lax.all_gather(targets, "ctx", axis=0, tiled=True),
        lax.all_gather(loss_mask, "ctx", axis=0, tiled=True),
    )
    raw_logits = jnp.einsum(
        "td,vd->tv",
        lax.all_gather(normed_full, "ctx", axis=0, tiled=True),
        embedding,
        preferred_element_type=jnp.float32,
    )
    logits = logit_cap * jnp.tanh(raw_logits / logit_cap)
    vocab_local = embedding.shape[0]
    vocab_base = (ctx_index * lax.axis_size("vocab") + lax.axis_index("vocab")) * vocab_local
    onehot = (vocab_base + jnp.arange(vocab_local, dtype=jnp.int32))[None, :] == all_targets[
        :, None
    ]
    exp_logits = jnp.exp(logits)
    local_total = jnp.sum(exp_logits, axis=1)
    local_target = jnp.sum(jnp.where(onehot, logits, 0.0), axis=1)
    totals, target_logit = lax.psum((local_total, local_target), ("ctx", "vocab"))
    mask_float = all_mask.astype(jnp.float32)
    mean_loss = jnp.sum(mask_float * (jnp.log(totals) - target_logit)) / all_targets.shape[0]
    dlogits = mask_float[:, None] * (exp_logits / totals[:, None] - onehot.astype(jnp.float32))
    dlogits = (dlogits * (1.0 - (logits / logit_cap) ** 2)).astype(jnp.bfloat16)
    partial_grad = jnp.dot(dlogits, embedding, preferred_element_type=jnp.float32)
    by_features = lax.psum_scatter(partial_grad, "vocab", scatter_dimension=1, tiled=True)
    grad_normed = lax.psum_scatter(by_features, "ctx", scatter_dimension=0, tiled=True)
    return (final_hidden, mean_loss, grad_normed)


def flip(index, offset):
    moved, bit = 0, 1
    while bit <= offset or bit == 1:
        here = lax.rem(index // bit, 2)
        moved = moved + bit * (lax.rem(here + (offset // bit) % 2, 2) - here)
        bit *= 2
    return index + moved


def fused_kernel(
    n, vn, q, k, v, res, w_hbm, post, gains, e_hbm, tm, pos,
    hid_out, loss_out, grad_out,
    q_all, k_all, v_all, out_all, att, w_buf, e_buf, part, own, up, down, sq_all, pick_z, gain_z, res_z, pk_send, pk_recv,
    pick_all, tm_all, tot_z, tot_p, gsend, grecv, zsend, zrecv, acc,
    w_sem, e_sem, qs, qr, ks, kr, vs, vr, fks, fkr, fvs, fvr, outs, outr, ups, upr, dns, dnr,
    sqs, sqr, pzs, pzr, gns, gnr, pas, par, tms, tmr, tzs, tzr, tps, tpr, gs, gr, zs, zr, rzs, rzr, pks, pkr,
):
    me, z = lax.axis_index("ctx"), lax.axis_index("vocab")
    tok, feat = res.shape
    model = vn * feat
    half = model // 2
    picks = tm.shape[0]
    total_picks = n * picks
    vocab_local = e_buf.shape[0]
    chunks = ups.shape[1]
    rows = tok // chunks
    f32 = jnp.float32

    def plane(i):
        return {"ctx": i, "vocab": z}

    def column(i):
        return {"ctx": me, "vocab": i}

    def copy(src, dst, send, recv, device):
        return pltpu.make_async_remote_copy(
            src_ref=src, dst_ref=dst, send_sem=send, recv_sem=recv,
            device_id=device, device_id_type=MESH,
        )

    def lanes(i):
        return pl.ds(pl.multiple_of(i * HEAD_DIM, HEAD_DIM), HEAD_DIM)

    barrier = pltpu.get_barrier_semaphore()
    for off in range(1, n):
        pl.semaphore_signal(barrier, inc=1, device_id=plane(flip(me, off)), device_id_type=MESH)
    for off in range(1, vn):
        pl.semaphore_signal(
            barrier, inc=1, device_id=column(lax.rem(z + off, vn)), device_id_type=MESH
        )
    w_copy = pltpu.make_async_copy(w_hbm, w_buf, w_sem)
    w_copy.start()
    chip = me // 2
    sibling = flip(me, 1)
    q_all[pl.ds(me, 1)] = q[:, lanes(me)][None]
    k_all[pl.ds(me, 1)] = k[:, lanes(chip)][None]
    v_all[pl.ds(me, 1)] = v[:, lanes(chip)][None]
    pl.semaphore_wait(barrier, n + vn - 2)

    kv_copies, q_copies, small = {}, {}, []
    for off in (*range(2, n, 2), 1):
        peer = flip(me, off)
        kv_copies[off] = (
            copy(k.at[:, lanes(peer // 2)], k_all.at[me], ks.at[off], kr.at[off], plane(peer)),
            copy(v.at[:, lanes(peer // 2)], v_all.at[me], vs.at[off], vr.at[off], plane(peer)),
        )
        for c in kv_copies[off]:
            c.start()
    for off in range(1, n):
        peer = flip(me, off)
        c = copy(q.at[:, lanes(peer)], q_all.at[me], qs.at[off], qr.at[off], plane(peer))
        c.start()
        q_copies[off] = c
    e_copy = pltpu.make_async_copy(e_hbm, e_buf, e_sem)
    e_copy.start()
    for off in range(1, n):
        peer = flip(me, off)
        c = copy(tm, tm_all.at[me], tms.at[off], tmr.at[off], plane(peer))
        c.start()
        small.append(c)
    for off in range(1, vn):
        c = copy(gains, gain_z.at[z], gns.at[off], gnr.at[off], column(lax.rem(z + off, vn)))
        c.start()
        small.append(c)
    tm_all[pl.ds(me, 1)] = tm[...][None]
    gain_z[pl.ds(z, 1)] = gains[...][None]
    chosen = pos[...] == lax.broadcasted_iota(jnp.int32, (picks, tok), 1)
    chosen = chosen.astype(f32).astype(jnp.bfloat16)
    res_z[pl.ds(z, 1)] = jnp.dot(chosen, res[...], preferred_element_type=f32)[None]
    for off in range(1, vn):
        c = copy(
            res_z.at[z], res_z.at[z], rzs.at[off], rzr.at[off], column(lax.rem(z + off, vn))
        )
        c.start()
        small.append(c)
    forwards = []
    for off in range(2, n, 2):
        source = flip(me, off)
        for c in kv_copies[off]:
            c.wait_recv()
        pair = (
            copy(k_all.at[source], k_all.at[source], fks.at[off], fkr.at[off], plane(sibling)),
            copy(v_all.at[source], v_all.at[source], fvs.at[off], fvr.at[off], plane(sibling)),
        )
        for c in pair:
            c.start()
        forwards.extend(pair)
    for c in kv_copies[1]:
        c.wait_recv()
    for off in range(1, n):
        q_copies[off].wait_recv()
    for c in forwards:
        c.wait_recv()

    row_id = lax.broadcasted_iota(jnp.int32, (tok, tok), 0)
    col_id = lax.broadcasted_iota(jnp.int32, (tok, tok), 1)
    causal = row_id >= col_id
    pre = query_scalar ** (-0.5) / attn_cap
    post_scale = attn_cap * math.log2(math.e)

    def out_copy(i):
        return copy(out_all.at[i], att.at[:, lanes(me)], outs.at[i], outr.at[me], plane(i))

    for i in range(n - 1, -1, -1):
        query = q_all[i]
        total = jnp.zeros((tok, 1), f32)
        values = jnp.zeros((tok, HEAD_DIM), f32)
        for j in range(i + 1):
            s = lax.dot_general(
                query, k_all[j], (((1,), (1,)), ((), ())), preferred_element_type=f32
            )
            w = jnp.exp2(jnp.tanh(s * pre) * post_scale)
            if j == i:
                w = jnp.where(causal, w, 0.0)
            total = total + jnp.sum(w, axis=1, keepdims=True)
            values = values + jnp.dot(w.astype(jnp.bfloat16), v_all[j], preferred_element_type=f32)
        out_all[i] = (values / total).astype(jnp.bfloat16)

        @pl.when(me == i)
        def _():
            att[:, i * HEAD_DIM : (i + 1) * HEAD_DIM] = out_all[i]

        @pl.when(me != i)
        def _():
            out_copy(i).start()

    w_copy.wait()
    for i in range(n):

        @pl.when(me != i)
        def _():
            copy(
                out_all.at[i], att.at[:, lanes(i)], outs.at[i], outr.at[i], plane(i)
            ).wait_recv()

    def up_copy(dst, r, source):
        at = pl.ds(r * rows, rows)
        return copy(
            source.at[dst, at], up.at[dst, at], ups.at[dst, r], upr.at[dst, r],
            column(jnp.minimum(z + 1, vn - 1)),
        )

    def down_copy(dst, r, source):
        at = pl.ds(r * rows, rows)
        return copy(
            source.at[dst, at], down.at[dst, at], dns.at[dst, r], dnr.at[dst, r],
            column(jnp.maximum(z - 1, 0)),
        )

    order = []
    for t in range(vn):
        for d in (vn - 1 - t, t):
            if d not in order:
                order.append(d)
    att_pick = jnp.dot(chosen, att[...], preferred_element_type=f32).astype(jnp.bfloat16)
    for dst in order:
        pk_send[dst] = jnp.dot(
            att_pick, w_buf[:, dst * feat : (dst + 1) * feat], preferred_element_type=f32
        )
    pk_copies = []
    for off in range(1, vn):
        peer = lax.rem(z + off, vn)
        c = copy(pk_send.at[peer], pk_recv.at[z], pks.at[off], pkr.at[off], column(peer))
        c.start()
        pk_copies.append(c)
    pk_recv[pl.ds(z, 1)] = pk_send[pl.ds(z, 1)]
    count = (vn - 1) * chunks
    shares = (1, 2, 5, 6, 9, 12)

    def sent(point):
        if point < 0:
            return 0
        if point >= len(shares):
            return count
        return count * shares[point] // shares[-1]

    def move(level, index):
        t, r = index // chunks, index % chunks
        at = pl.ds(r * rows, rows)
        if t >= vn - 1 - level:
            return
        for here, dst, buffer, link in (
            (level, vn - 1 - t, up, up_copy),
            (vn - 1 - level, t, down, down_copy),
        ):

            @pl.when(z == here)
            def _():
                if level == 0:
                    link(dst, r, part).start()
                else:
                    link(dst, r, buffer).wait_recv()
                    buffer[dst, at] = (
                        buffer[dst, at].astype(f32) + part[dst, at].astype(f32)
                    ).astype(jnp.bfloat16)
                    link(dst, r, buffer).start()

    def advance(point):
        for level in range(vn - 1):
            for index in range(sent(point - level - 1), sent(point - level)):
                move(level, index)

    for dst in order:
        product = jnp.dot(
            att[...], w_buf[:, dst * feat : (dst + 1) * feat], preferred_element_type=f32
        )

        @pl.when(z == dst)
        def _():
            own[...] = product

        @pl.when(z != dst)
        def _():
            part[dst] = product.astype(jnp.bfloat16)

    advance(0)
    for c in pk_copies:
        c.wait_recv()
    pick_z[pl.ds(z, 1)] = jnp.sum(pk_recv[...], axis=0)[None]
    pz_copies = []
    for off in range(1, vn):
        c = copy(
            pick_z.at[z], pick_z.at[z], pzs.at[off], pzr.at[off], column(lax.rem(z + off, vn))
        )
        c.start()
        pz_copies.append(c)
    advance(1)
    for c in small:
        c.wait_recv()
    for c in pz_copies:
        c.wait_recv()
    proj = jnp.concatenate([pick_z[i] for i in range(vn)], axis=1)
    gain = jnp.concatenate([gain_z[i, :picks] for i in range(vn)], axis=1)
    gain_post = jnp.concatenate([gain_z[i, picks:] for i in range(vn)], axis=1)
    res_pick = jnp.concatenate([res_z[i] for i in range(vn)], axis=1)
    scale = lax.rsqrt(jnp.sum(proj * proj, axis=1, keepdims=True) / model + epsilon)
    whole = (res_pick + proj * scale * gain_post).astype(jnp.bfloat16).astype(f32)
    scale = lax.rsqrt(jnp.sum(whole * whole, axis=1, keepdims=True) / model + epsilon)
    normed = whole * scale * gain
    pick_all[pl.ds(me, 1)] = (
        jnp.concatenate([normed[:, :half], normed[:, half:]], axis=0).astype(jnp.bfloat16)[None]
    )
    pa_copies = {}
    for off in (*range(2, n, 2), 1):
        pa_copies[off] = copy(
            pick_all.at[me], pick_all.at[me], pas.at[off], par.at[off], plane(flip(me, off))
        )
        pa_copies[off].start()
    advance(2)
    passed = []
    for off in range(2, n, 2):
        source = flip(me, off)
        pa_copies[off].wait_recv()
        c = copy(
            pick_all.at[source], pick_all.at[source], pas.at[off + 1], par.at[off + 1],
            plane(sibling),
        )
        c.start()
        passed.append(c)
    pa_copies[1].wait_recv()
    for c in passed:
        c.wait_recv()
    e_copy.wait()
    left, right = [], []
    for i in range(n):
        block = pick_all[i].astype(f32)
        left.append(block[:picks])
        right.append(block[picks:])
    states = jnp.concatenate(
        [jnp.concatenate(left, axis=0), jnp.concatenate(right, axis=0)], axis=1
    ).astype(jnp.bfloat16)
    raw = lax.dot_general(
        states, e_buf[...], (((1,), (1,)), ((), ())), preferred_element_type=f32
    )
    ratio = jnp.tanh(raw / logit_cap)
    logits = logit_cap * ratio
    tm_rows = tm_all[...].reshape(total_picks, 128)
    target = tm_rows[:, :1]
    mask = tm_rows[:, 64:65].astype(f32)
    base = (me * vn + z) * vocab_local
    onehot = base + lax.broadcasted_iota(jnp.int32, (total_picks, vocab_local), 1) == target
    exp_logits = jnp.exp(logits)
    slope = 1.0 - ratio * ratio
    local_total = jnp.sum(exp_logits, axis=1, keepdims=True)
    local_target = jnp.sum(jnp.where(onehot, logits, 0.0), axis=1, keepdims=True)
    target_slope = jnp.sum(jnp.where(onehot, slope, 0.0), axis=1, keepdims=True)
    target_exp = jnp.sum(jnp.where(onehot, exp_logits, 0.0), axis=1, keepdims=True)
    lane = lax.broadcasted_iota(jnp.int32, (total_picks, 128), 1)
    packed = jnp.where(lane == 0, local_total, jnp.where(lane == 1, local_target, 0.0))
    packed = jnp.concatenate([packed, jnp.zeros((128 - total_picks, 128), f32)], axis=0)
    tot_z[pl.ds(z, 1)] = jnp.transpose(packed)[:8][None]
    tz_copies = []
    for off in range(1, vn):
        c = copy(tot_z.at[z], tot_z.at[z], tzs.at[off], tzr.at[off], column(lax.rem(z + off, vn)))
        c.start()
        tz_copies.append(c)
    advance(3)
    weights = jnp.concatenate(
        [jnp.where(onehot, 0.0, exp_logits * slope), jnp.where(onehot, 1.0, 0.0)], axis=0
    ).astype(jnp.bfloat16)
    for c in tz_copies:
        c.wait_recv()
    tot_p[pl.ds(me, 1)] = jnp.sum(tot_z[...], axis=0)[None]
    tp_copies = []
    for off in range(1, n):
        c = copy(tot_p.at[me], tot_p.at[me], tps.at[off], tpr.at[off], plane(flip(me, off)))
        c.start()
        tp_copies.append(c)
    acc[...] = jnp.dot(weights, e_buf[...], preferred_element_type=f32)
    for c in tp_copies:
        c.wait_recv()
    sums = jnp.sum(tot_p[...], axis=0)
    sums = jnp.transpose(jnp.concatenate([sums, jnp.zeros((120, 128), f32)], axis=0))
    totals = sums[:total_picks, :1]
    target_logit = sums[:total_picks, 1:2]
    loss = jnp.sum(mask * (jnp.log(totals) - target_logit), axis=0, keepdims=True) / total_picks
    loss_out[...] = jnp.broadcast_to(loss, loss_out.shape)
    other = mask / totals
    at_target = (mask * (target_exp / totals - 1.0) * target_slope).astype(jnp.bfloat16).astype(f32)
    grad = other * acc[:total_picks] + at_target * acc[total_picks:]
    for i in range(n):
        block = grad[i * picks : (i + 1) * picks]
        gsend[i] = jnp.concatenate([block[:, :half], block[:, half:]], axis=0).astype(jnp.bfloat16)
    g_copies = []
    for off in (*range(2, n), 1):
        peer = flip(me, off)
        c = copy(gsend.at[peer], grecv.at[me], gs.at[off], gr.at[off], plane(peer))
        c.start()
        g_copies.append(c)
    grecv[pl.ds(me, 1)] = gsend[pl.ds(me, 1)]
    advance(4)
    for c in g_copies:
        c.wait_recv()
    both = grecv[0].astype(f32)
    for i in range(1, n):
        both = both + grecv[i].astype(f32)
    mine = jnp.concatenate([both[:picks], both[picks:]], axis=1)
    for i in range(vn):
        zsend[i] = mine[:, i * feat : (i + 1) * feat]
    z_copies = []
    for off in range(1, vn):
        peer = lax.rem(z + off, vn)
        c = copy(zsend.at[peer], zrecv.at[z], zs.at[off], zr.at[off], column(peer))
        c.start()
        z_copies.append(c)
    zrecv[pl.ds(z, 1)] = zsend[pl.ds(z, 1)]
    for point in range(5, len(shares) + vn - 1):
        advance(point)
    for dst in range(vn):

        @pl.when(z == dst)
        def _():
            for r in range(chunks):
                at = pl.ds(r * rows, rows)
                value = own[at]
                if dst > 0:
                    up_copy(dst, r, up).wait_recv()
                    value = value + up[dst, at].astype(f32)
                if dst < vn - 1:
                    down_copy(dst, r, down).wait_recv()
                    value = value + down[dst, at].astype(f32)
                own[at] = value

    cols = own[...]
    squares = jnp.sum(cols * cols, axis=1, keepdims=True)
    wide = jnp.transpose(jnp.broadcast_to(squares, (tok, 128)))
    sq_all[pl.ds(z, 1)] = wide[:8][None]
    sq_copies = []
    for off in range(1, vn):
        c = copy(
            sq_all.at[z], sq_all.at[z], sqs.at[off], sqr.at[off], column(lax.rem(z + off, vn))
        )
        c.start()
        sq_copies.append(c)
    for c in sq_copies:
        c.wait_recv()
    summed = jnp.sum(sq_all[...], axis=0)[:1]
    inv = lax.rsqrt(summed / model + epsilon)
    inv = jnp.transpose(jnp.broadcast_to(inv, (128, tok)))[:, :1]
    hidden = (res[...].astype(f32) + cols * inv * post[...]).astype(jnp.bfloat16)
    hid_out[...] = hidden
    for c in z_copies:
        c.wait_recv()
    grad_out[...] = jnp.sum(zrecv[...], axis=0)

    for pair in kv_copies.values():
        for c in pair:
            c.wait_send()
    for group in (
        q_copies.values(), small, forwards, sq_copies, pk_copies, pz_copies, pa_copies.values(), passed,
        tz_copies, tp_copies, g_copies, z_copies,
    ):
        for c in group:
            c.wait_send()
    for i in range(n):

        @pl.when(me != i)
        def _():
            out_copy(i).wait_send()

    for dst in range(vn):
        for r in range(chunks):

            @pl.when(z < dst)
            def _():
                up_copy(dst, r, up).wait_send()

            @pl.when(z > dst)
            def _():
                down_copy(dst, r, down).wait_send()


def fused(
    n, vn, query_rows, key_rows, value_rows, residual, out_weight, post_gain, final_gain,
    embedding, targets, loss_mask, pick_pos,
):
    tok, feat = residual.shape
    model = vn * feat
    picks = targets.shape[0]
    bf16, f32, i32 = jnp.bfloat16, jnp.float32, jnp.int32
    chunks = 4
    first = jnp.broadcast_to(targets[:, None], (picks, 64))
    second = jnp.broadcast_to(loss_mask[:, None], (picks, 64))
    tm = jnp.concatenate([first, second], axis=1)
    gains = jnp.concatenate(
        [jnp.broadcast_to(g[None, :], (picks, feat)) for g in (final_gain, post_gain)], axis=0
    )
    dma = pltpu.SemaphoreType.DMA
    vmem = pl.BlockSpec(memory_space=pltpu.VMEM)
    hbm = pl.BlockSpec(memory_space=pl.ANY)
    sems = [dma, dma] + [dma((n,))] * 12 + [dma((vn, chunks))] * 4 + [dma((vn,))] * 6
    sems += [dma((n,))] * 4 + [dma((vn,))] * 2 + [dma((n,))] * 4 + [dma((vn,))] * 6
    hidden, loss, grad = pl.pallas_call(
        functools.partial(fused_kernel, n, vn),
        out_shape=(
            jax.ShapeDtypeStruct((tok, feat), bf16),
            jax.ShapeDtypeStruct((8, 128), f32),
            jax.ShapeDtypeStruct((picks, feat), f32),
        ),
        in_specs=[vmem, vmem, vmem, vmem, hbm, vmem, vmem, hbm, vmem, vmem],
        out_specs=(vmem, vmem, vmem),
        scratch_shapes=[
            pltpu.VMEM((n, tok, HEAD_DIM), bf16),
            pltpu.VMEM((n, tok, HEAD_DIM), bf16),
            pltpu.VMEM((n, tok, HEAD_DIM), bf16),
            pltpu.VMEM((n, tok, HEAD_DIM), bf16),
            pltpu.VMEM((tok, n * HEAD_DIM), bf16),
            pltpu.VMEM(out_weight.shape, bf16),
            pltpu.VMEM(embedding.shape, bf16),
            pltpu.VMEM((vn, tok, feat), bf16),
            pltpu.VMEM((tok, feat), f32),
            pltpu.VMEM((vn, tok, feat), bf16),
            pltpu.VMEM((vn, tok, feat), bf16),
            pltpu.VMEM((vn, 8, tok), f32),
            pltpu.VMEM((vn, picks, feat), f32),
            pltpu.VMEM((vn, 2 * picks, feat), f32),
            pltpu.VMEM((vn, picks, feat), f32),
            pltpu.VMEM((vn, picks, feat), f32),
            pltpu.VMEM((vn, picks, feat), f32),
            pltpu.VMEM((n, 2 * picks, model // 2), bf16),
            pltpu.VMEM((n, picks, 128), i32),
            pltpu.VMEM((vn, 8, 128), f32),
            pltpu.VMEM((n, 8, 128), f32),
            pltpu.VMEM((n, 2 * picks, model // 2), bf16),
            pltpu.VMEM((n, 2 * picks, model // 2), bf16),
            pltpu.VMEM((vn, picks, feat), f32),
            pltpu.VMEM((vn, picks, feat), f32),
            pltpu.VMEM((2 * n * picks, model), f32),
            *sems,
        ],
        compiler_params=pltpu.CompilerParams(
            collective_id=0, has_side_effects=True, vmem_limit_bytes=60 * 1024 * 1024
        ),
    )(
        query_rows, key_rows, value_rows, residual, out_weight, post_gain[None, :],
        gains, embedding, tm, pick_pos[:, None],
    )
    return hidden, loss[0, 0], grad


def fits(n, vn, query_rows, key_rows, residual, targets):
    heads, kv = query_rows.shape[1] // HEAD_DIM, key_rows.shape[1] // HEAD_DIM
    tok, feat = residual.shape
    return (
        n >= 2
        and n & (n - 1) == 0
        and heads == n
        and heads == 2 * kv
        and vn >= 2
        and n * tok <= WINDOW
        and tok % 128 == 0
        and feat % 128 == 0
        and (vn * feat) % 256 == 0
        and targets.shape[0] == 8
        and n * targets.shape[0] <= 128
    )


def solution(mesh):
    in_specs = (
        P("ctx", "vocab"),
        P("ctx", "vocab"),
        P("ctx", "vocab"),
        P("ctx", "vocab"),
        P("vocab", None),
        P("vocab"),
        P("vocab"),
        P(("ctx", "vocab"), None),
        P("ctx"),
        P("ctx"),
        P("ctx"),
    )
    out_specs = (P("ctx", "vocab"), P(), P("ctx", "vocab"))
    n, vn = mesh.shape["ctx"], mesh.shape["vocab"]

    def local(*args):
        if fits(n, vn, args[0], args[1], args[3], args[8]):
            return fused(n, vn, *args)
        return shards(*args)

    return jax.shard_map(local, mesh=mesh, in_specs=in_specs, out_specs=out_specs, check_vma=False)
```
